256 devices in a mesh: tm: 8 (over x, z_lo), row: 4 (over z_hi), head: 8 (over y, core).
Axes of the slice: x: 4, y: 4, z: 8 (z_hi: 4, z_lo: 2; z = z_hi * 2 + z_lo), core: 2. Of those that a mesh axis runs over, the one named last changes fastest.
Arguments:
- query: bfloat16 [8, 4, 2, 384, 3072], P('tm', 'row', None, None, 'head'), may hold values from -8 to 8
- key_tiles: bfloat16 [8, 4, 2, 384, 3072], P('tm', 'row', None, None, 'head'), may hold values from -8 to 8
- value_tiles: bfloat16 [8, 4, 2, 384, 3072], P('tm', 'row', None, None, 'head'), may hold values from -6 to 6
- grad_out: bfloat16 [8, 4, 2, 384, 3072], P('tm', 'row', None, None, 'head'), may hold values from -24 to 24
- neighbours: int32 [8, 4, 2, 8], P('tm', 'row'), may hold values from -1 to 17, as said below
Outputs:
- grad_query: bfloat16 [8, 4, 2, 384, 3072], P('tm', 'row', None, None, 'head')
- grad_key: bfloat16 [8, 4, 2, 384, 3072], P('tm', 'row', None, None, 'head')
- grad_value: bfloat16 [8, 4, 2, 384, 3072], P('tm', 'row', None, None, 'head')
The draws below stay inside these ranges and needn't reach their ends.
Inputs may be any that keep to these rules, and one draw needn't show every extreme that they name: `neighbours`: entry n of a tile's list at time block t and row block r is (3 * (dt + 1) + (dr + 1)) * 2 + j with dt, dr in -1, 0, 1 such that time block t + dt and row block r + dr exist; entry 0 names the tile itself; the named values of one list are distinct; entries equal to -1 are unused and stand after all used ones; the number of used entries is the smaller of 8 and 2 times the number of existing blocks among the nine around (t, r).
All inputs are finite; a program needn't handle non-finite values.
Results may differ from the reference program's by a relative error of at most 0.0078.
Values may be sent and summed in bfloat16 or wider, within the bound.
A program may use at most 128 MiB of HBM per device.

```python
from functools import partial
import jax
import jax.numpy as jnp
from jax import lax

HEADS = 24
HD = 128
TILE_TOKENS = 384
NBR = 8
TD = 2
TIME_BLOCKS = 8
ROW_BLOCKS = 4


def tile_shape():
    return (TIME_BLOCKS, ROW_BLOCKS, TD, TILE_TOKENS, HEADS * HD)


def base_field(key, salt, spread):
    return jnp.clip(spread * jax.random.normal(jax.random.fold_in(key, salt), tile_shape(), jnp.float32), -8.0, 8.0)


def draw_query(key, part):
    field = base_field(key, 11, 2.0)
    return field.astype(jnp.bfloat16)


def draw_key_tiles(key, part):
    field = base_field(key, 13, 1.0)
    return field.astype(jnp.bfloat16)


def draw_neighbours(key, part):
    key = jax.random.fold_in(key, 41)
    slot_count = 9 * TD
    time_pos = jnp.arange(TIME_BLOCKS)[:, None, None, None]
    row_pos = jnp.arange(ROW_BLOCKS)[None, :, None, None]
    tile_pos = jnp.arange(TD)[None, None, :, None]
    slot_ids = jnp.arange(slot_count)[None, None, None, :]
    code = slot_ids // TD
    time_off = code // 3 - 1
    row_off = code % 3 - 1
    valid = (time_pos + time_off >= 0) & (time_pos + time_off < TIME_BLOCKS) & (row_pos + row_off >= 0) & (row_pos + row_off < ROW_BLOCKS)
    own_slot = slot_ids == 4 * TD + tile_pos
    noise = jax.random.randint(key, (TIME_BLOCKS, ROW_BLOCKS, TD, slot_count), 0, 1 << 20)
    ranking = jnp.where(own_slot, 0, jnp.where(valid, noise + 1, 1 << 21)) * 256 + slot_ids
    order = jnp.argsort(ranking, axis=-1, stable=True)[..., :NBR]
    valid_count = jnp.sum(valid.astype(jnp.int32), axis=-1, keepdims=True)
    entry_pos = jnp.arange(NBR)
    used = entry_pos < valid_count
    return jnp.where(used, order, -1).astype(jnp.int32)


def block_scale(rng, dims, cuts, low, largest):
    def one(dim, blocks):
        steps = jax.random.uniform(jax.random.fold_in(jax.random.fold_in(rng, 6), dim), (blocks,), jnp.float32, low / len(cuts), largest / len(cuts))
        return jnp.repeat(jnp.exp(steps), dims[dim] // blocks).reshape((-1,) + (1,) * (len(dims) - dim - 1))

    gain = one(*cuts[0])
    for cut in cuts[1:]:
        gain = gain * one(*cut)
    return gain


def centred(stream_key, extent, scale, reach, shards=(), kind=jnp.bfloat16):
    gain = block_scale(stream_key, extent, shards, -0.22, 0.18) if shards else 1.0
    values = jax.random.normal(stream_key, extent, jnp.float32) * scale * gain
    return jnp.minimum(jnp.maximum(values, -reach), reach).astype(kind)


def setup_inputs(seed: int = 0) -> dict:
    key_of = jax.random.split(jax.random.key(seed), 6)
    return {
        "query": draw_query(jax.random.fold_in(key_of[5], 71), 0),
        "key_tiles": draw_key_tiles(jax.random.fold_in(key_of[5], 71), 0),
        "value_tiles": centred(key_of[2], (TIME_BLOCKS, ROW_BLOCKS, TD, TILE_TOKENS, HEADS * HD), 1.0, 6.0, ((0, 8), (1, 4), (4, 8))),
        "grad_out": centred(key_of[3], (TIME_BLOCKS, ROW_BLOCKS, TD, TILE_TOKENS, HEADS * HD), 4.0, 24.0, ((0, 8), (1, 4), (4, 8))),
        "neighbours": draw_neighbours(jax.random.fold_in(key_of[5], 71), 0),
    }


def lowered(values):
    return lax.optimization_barrier(values.astype(jnp.bfloat16)).astype(jnp.float32)


def tile_backward(running, inputs, key_head, value_head, score_scale):
    query_tile, grad_tile, entries = inputs
    slot_count = key_head.shape[0]
    is_live = entries >= 0
    picked = jnp.maximum(entries, 0)
    keys_used = key_head[picked]
    values_used = value_head[picked]
    scores = jnp.einsum("qd,nkd->qnk", query_tile, keys_used) * score_scale
    scores = jnp.where(is_live[None, :, None], scores, -1e30)
    row_peak = jnp.max(scores, axis=(1, 2), keepdims=True)
    log_total = row_peak + jnp.log(jnp.sum(jnp.exp(scores - row_peak), axis=(1, 2), keepdims=True))
    attn_probs = jnp.exp(scores - log_total)
    grad_probs = jnp.einsum("qd,nkd->qnk", grad_tile, values_used)
    row_delta = jnp.sum(attn_probs * grad_probs, axis=(1, 2), keepdims=True)
    grad_scores = attn_probs * (grad_probs - row_delta)
    low_probs = lowered(attn_probs)
    low_grads = lowered(grad_scores)
    grad_query = jnp.einsum("qnk,nkd->qd", low_grads, keys_used) * score_scale
    value_terms = jnp.einsum("qnk,qd->nkd", low_probs, grad_tile)
    key_terms = jnp.einsum("qnk,qd->nkd", low_grads, query_tile) * score_scale
    selector = (entries[:, None] == jnp.arange(slot_count, dtype=jnp.int32)[None, :]).astype(jnp.float32)
    key_sum = running[0] + jnp.einsum("ns,nkd->skd", selector, key_terms, precision=lax.Precision.HIGHEST)
    value_sum = running[1] + jnp.einsum("ns,nkd->skd", selector, value_terms, precision=lax.Precision.HIGHEST)
    return (key_sum, value_sum), grad_query


def slot_view(field):
    time_blocks, row_blocks, tile_count, tile_len, head_width = field.shape
    padded = jnp.pad(field, ((1, 1), (1, 1), (0, 0), (0, 0), (0, 0)))
    pieces = [padded[time_off:time_off + time_blocks, row_off:row_off + row_blocks] for time_off in range(3) for row_off in range(3)]
    stacked = jnp.stack(pieces, axis=2)
    return stacked.reshape(time_blocks, row_blocks, 9 * tile_count, tile_len, head_width)


def collect(parts):
    time_blocks, row_blocks = parts.shape[0], parts.shape[1]
    totals = jnp.zeros((time_blocks + 2, row_blocks + 2) + parts.shape[4:], jnp.float32)
    for time_off in range(3):
        for row_off in range(3):
            totals = totals.at[time_off:time_off + time_blocks, row_off:row_off + row_blocks].add(parts[:, :, time_off, row_off])
    return totals[1:-1, 1:-1]


def reference(query, key_tiles, value_tiles, grad_out, neighbours):
    time_blocks, row_blocks, tile_count, tile_len, channels = query.shape
    slot_count = 9 * tile_count
    score_scale = HD ** -0.5
    device_count = time_blocks * row_blocks

    def flatten(field):
        return field.reshape((device_count,) + field.shape[2:])

    def one_head(head_index):
        def take(field):
            return lax.dynamic_slice_in_dim(field, head_index * HD, HD, 4).astype(jnp.float32)

        query_head = take(query)
        grad_head = take(grad_out)
        key_view = slot_view(take(key_tiles))
        value_view = slot_view(take(value_tiles))

        def one_device(query_dev, grad_dev, entry_dev, key_dev, value_dev):
            zeros = jnp.zeros((slot_count, tile_len, HD), jnp.float32)
            stepper = partial(tile_backward, key_head=key_dev, value_head=value_dev, score_scale=score_scale)
            sums, grads = lax.scan(stepper, (zeros, zeros), (query_dev, grad_dev, entry_dev))
            return grads, sums[0], sums[1]

        grads, key_sums, value_sums = jax.vmap(one_device)(flatten(query_head), flatten(grad_head), flatten(neighbours), flatten(key_view), flatten(value_view))
        part_shape = (time_blocks, row_blocks, 3, 3, tile_count, tile_len, HD)
        grad_key = collect(lowered(key_sums).reshape(part_shape))
        grad_value = collect(lowered(value_sums).reshape(part_shape))
        grad_query = grads.reshape(time_blocks, row_blocks, tile_count, tile_len, HD)
        return grad_query.astype(jnp.bfloat16), grad_key.astype(jnp.bfloat16), grad_value.astype(jnp.bfloat16)

    stacked = lax.map(one_head, jnp.arange(HEADS, dtype=jnp.int32))

    def merge_heads(field):
        return jnp.moveaxis(field, 0, 4).reshape(time_blocks, row_blocks, tile_count, tile_len, channels)

    return (merge_heads(stacked[0]), merge_heads(stacked[1]), merge_heads(stacked[2]))
```

```python
import functools

import jax
import jax.numpy as jnp
from jax import lax
from jax.experimental import pallas as pl
from jax.experimental.pallas import tpu as pltpu
from jax.sharding import PartitionSpec as P

HD = 128
SLOTS = 9
UNUSED = 1e30
SAME_M, OWN, SAME_P, OTHER_M, OTHER_0, OTHER_P, CROSS_M, CROSS_0, CROSS_P = range(9)
FIRST_ORDER = (OWN, OTHER_0, OTHER_M, SAME_M, SAME_P, OTHER_P, CROSS_0, CROSS_M, CROSS_P)
SECOND_ORDER = (CROSS_P, CROSS_M, CROSS_0, SAME_P, OTHER_P, SAME_M, OTHER_M, OTHER_0, OWN)
SEND_OWN, RELAY_1, RELAY_2, RELAY_3 = 0, 3, 6, 9
FIRST = 13
MERGE = FIRST + 10
SECOND = FIRST + 13
RET_OTHER_P = SECOND + 5
RET_OTHER_M = SECOND + 7
RET_SAME_M = SECOND + 8
RET_OTHER_0 = SECOND + 11
RET_OWN = SECOND + 14
MESH = pl.DeviceIdType.MESH


def mirror(slot):
    return 2 - slot if slot < 3 else slot


def pick(table, index):
    value = jnp.int32(table[0])
    for k in range(1, len(table)):
        value = jnp.where(index == k, jnp.int32(table[k]), value)
    return value


def dot(a, b, dims):
    return lax.dot_general(a, b, (dims, ((), ())), preferred_element_type=jnp.float32)


def kernel(times, rows, heads, tile, q_hbm, k_hbm, v_hbm, g_hbm, mask, dq_hbm, dk_hbm, dv_hbm,
           fwd, keys, vals, keys_t, acc_k, acc_v, part, ret_out, ret_in, st_out, st_in, bc_out, bc_in,
           out_q, out_k, out_v, load_sem, fwd_s, fwd_r, st_s, st_r, bc_s, bc_r, ret_s, ret_r):
    chunk = fwd.shape[3]
    per_head = 2 * tile // chunk
    chunks = heads * per_head
    scale = HD ** -0.5
    scale2 = scale * 1.4426950408889634

    t, r = lax.axis_index("tm"), lax.axis_index("row")
    s = 1 - 2 * (t % 2)
    has_m = jnp.logical_and(r - s >= 0, r - s < rows)
    has_p = jnp.logical_and(r + s >= 0, r + s < rows)
    has_xo = jnp.logical_and(t + 2 * s >= 0, t + 2 * s < times)
    has_xi = jnp.logical_and(t - 2 * s >= 0, t - 2 * s < times)
    pair = {"tm": t + s, "row": r}
    outer = {"tm": t + s, "row": r - s}
    x_out = {"tm": t + 2 * s, "row": r}
    x_in = {"tm": t - 2 * s, "row": r}

    def both(a, b):
        return jnp.logical_and(a, b)

    row_ok = (has_m, True, has_p)

    def exists(slot):
        ok = row_ok[slot % 3]
        if slot // 3 == 2:
            ok = has_xi if ok is True else both(ok, has_xi)
        return ok

    def sent_to(slot):
        kind = (0, 1, -1)[slot // 3]
        return {"tm": t + s * kind, "row": r + s * (slot % 3 - 1)}

    def when(cond, fn):
        if cond is True:
            fn()
        else:
            pl.when(cond)(fn)

    loads = []
    for c in range(chunks):
        h, k = c // per_head, c % per_head
        for n, ref in enumerate((q_hbm, g_hbm)):
            loads.append(pltpu.make_async_copy(
                ref.at[pl.ds(k * chunk, chunk), pl.ds(h * HD, HD)], fwd.at[c, OWN, n], load_sem.at[len(loads)]))
    for h in range(heads):
        for ref, dst in ((k_hbm, keys), (v_hbm, vals)):
            loads.append(pltpu.make_async_copy(ref.at[:, pl.ds(h * HD, HD)], dst.at[h], load_sem.at[len(loads)]))
    for copy in loads:
        copy.start()

    barrier = pltpu.get_barrier_semaphore()
    greeted = [(sent_to(b), exists(b)) for b in range(SLOTS) if b != OWN] + [(x_out, has_xo), (x_in, has_xi)]
    count = jnp.int32(0)
    for device, ok in greeted:
        def greet(device=device):
            pl.semaphore_signal(barrier, inc=1, device_id=device, device_id_type=MESH)
        when(ok, greet)
        count = count + (1 if ok is True else ok.astype(jnp.int32))
    for copy in loads:
        copy.wait()
    for h in range(heads):
        keys_t[h] = keys[h].T
    acc_k[...] = jnp.zeros_like(acc_k)
    acc_v[...] = jnp.zeros_like(acc_v)
    pl.semaphore_wait(barrier, count)

    def fwd_copy(c, src, dst, device):
        return pltpu.make_async_remote_copy(
            src_ref=fwd.at[c, src], dst_ref=fwd.at[c, dst], send_sem=fwd_s.at[c, dst], recv_sem=fwd_r.at[c, dst],
            device_id=device, device_id_type=MESH)

    def st_copy(c, slot):
        return pltpu.make_async_remote_copy(
            src_ref=st_out.at[c, slot], dst_ref=st_in.at[c, mirror(slot)], send_sem=st_s.at[c, slot],
            recv_sem=st_r.at[c, mirror(slot)], device_id=sent_to(slot), device_id_type=MESH)

    def bc_copy(c, slot):
        return pltpu.make_async_remote_copy(
            src_ref=bc_out.at[c, slot], dst_ref=bc_in.at[c, mirror(slot)], send_sem=bc_s.at[c, slot],
            recv_sem=bc_r.at[c, mirror(slot)], device_id=sent_to(slot), device_id_type=MESH)

    def ret_copy(c, slot, device):
        return pltpu.make_async_remote_copy(
            src_ref=ret_out.at[c, slot], dst_ref=ret_in.at[c, slot], send_sem=ret_s.at[c, slot],
            recv_sem=ret_r.at[c, slot], device_id=device, device_id_type=MESH)

    def local_wait(buf, sems, c, slot):
        pltpu.make_async_copy(buf.at[c, slot], buf.at[c, slot], sems.at[c, slot]).wait()

    fwd_plan = (
        (OWN, OTHER_0, pair, True), (OWN, OTHER_M, outer, has_m),
        (OTHER_0, SAME_M, outer, has_m), (OTHER_0, CROSS_0, x_out, has_xo),
        (OTHER_M, SAME_P, pair, has_m), (OTHER_M, CROSS_M, x_out, both(has_m, has_xo)),
        (SAME_M, OTHER_P, pair, has_m), (OTHER_P, CROSS_P, x_out, both(has_p, has_xo)),
    )
    ret_device = {
        CROSS_P: x_in, CROSS_M: x_in, CROSS_0: x_in, SAME_P: pair, OTHER_P: pair,
        SAME_M: outer, OTHER_M: outer, OTHER_0: pair,
    }
    ret_adds = {
        OTHER_P: ((CROSS_P, has_xo),), SAME_M: ((OTHER_P, True),), OTHER_M: ((CROSS_M, has_xo), (SAME_P, True)),
        OTHER_0: ((CROSS_0, has_xo), (SAME_M, has_m)), OWN: ((OTHER_M, has_m), (OTHER_0, True)),
    }

    def send_fwd(c, src):
        for a, b, device, ok in fwd_plan:
            if a == src:
                when(ok, lambda a=a, b=b, device=device: fwd_copy(c, a, b, device).start())

    def relay(c, src):
        def go():
            local_wait(fwd, fwd_r, c, src)
            send_fwd(c, src)
        when(exists(src), go)

    def first_pass(c, slot):
        h = c // per_head
        q = fwd[c, slot, 0]
        g = fwd[c, slot, 1]
        for j in range(2):
            sc = dot(keys[h, pl.ds(j * tile, tile), :], q, ((1,), (1,)))
            peak = jnp.max(sc, axis=0, keepdims=True) * scale2
            e = jnp.exp2(sc * scale2 - peak)
            dp = dot(vals[h, pl.ds(j * tile, tile), :], g, ((1,), (1,)))
            st_out[c, slot, pl.ds(j, 1), :] = peak
            st_out[c, slot, pl.ds(2 + j, 1), :] = jnp.sum(e, axis=0, keepdims=True)
            st_out[c, slot, pl.ds(4 + j, 1), :] = jnp.sum(e * dp, axis=0, keepdims=True)

    def merge(c):
        for slot in range(SLOTS):
            if slot != OWN:
                when(exists(slot), lambda slot=slot: local_wait(st_in, st_r, c, slot))
        k = c % per_head

        def entry(slot, row):
            ref = st_out if slot == OWN else st_in
            return ref[c, slot, pl.ds(row, 2), :]

        used = [mask[k, slot, pl.ds(0, 2), :] > 0.5 for slot in range(SLOTS)]
        peaks = [jnp.where(used[slot], entry(slot, 0), -UNUSED) for slot in range(SLOTS)]
        top = functools.reduce(jnp.maximum, peaks)
        top = jnp.max(top, axis=0, keepdims=True)
        total = jnp.zeros_like(peaks[0])
        delta = jnp.zeros_like(peaks[0])
        for slot in range(SLOTS):
            w = jnp.exp2(peaks[slot] - top)
            total = total + jnp.where(used[slot], w * entry(slot, 2), 0.0)
            delta = delta + jnp.where(used[slot], w * entry(slot, 4), 0.0)
        total = jnp.sum(total, axis=0, keepdims=True)
        delta = jnp.sum(delta, axis=0, keepdims=True) / total
        lse = top + jnp.log2(total)
        for slot in range(SLOTS):
            ref = bc_in if slot == OWN else bc_out
            ref[c, slot, pl.ds(0, 2), :] = jnp.where(used[slot], lse, UNUSED)
            ref[c, slot, pl.ds(2, 1), :] = delta
        for slot in range(SLOTS):
            if slot != OWN:
                when(exists(slot), lambda slot=slot: bc_copy(c, slot).start())

    def second_pass(c, slot):
        h = c // per_head
        q = fwd[c, slot, 0]
        g = fwd[c, slot, 1]
        delta = bc_in[c, slot, pl.ds(2, 1), :]
        dq_t = None
        for j in range(2):
            span = pl.ds(j * tile, tile)
            sc = dot(keys[h, span, :], q, ((1,), (1,)))
            p = jnp.exp2(sc * scale2 - bc_in[c, slot, pl.ds(j, 1), :])
            dp = dot(vals[h, span, :], g, ((1,), (1,)))
            ds = (p * (dp - delta)).astype(jnp.bfloat16)
            acc_v[h, span, :] += dot(p.astype(jnp.bfloat16), g, ((1,), (0,)))
            acc_k[h, span, :] += dot(ds, q, ((1,), (0,)))
            term = dot(keys_t[h, :, span], ds, ((1,), (0,)))
            dq_t = term if dq_t is None else dq_t + term
        part[c % 2, slot] = dq_t

    def hand_back(c, slot):
        def go():
            for src, ok in ret_adds.get(slot, ()):
                def add(src=src):
                    local_wait(ret_in, ret_r, c, src)
                    part[c % 2, slot] += ret_in[c, src].astype(jnp.float32)
                when(ok, add)
            if slot == OWN:
                rows_at = pl.multiple_of((c % per_head) * chunk, chunk)
                out_q[c // per_head, pl.ds(rows_at, chunk), :] = (part[c % 2, slot] * scale).T.astype(jnp.bfloat16)
            else:
                ret_out[c, slot] = part[c % 2, slot].astype(jnp.bfloat16)
                ret_copy(c, slot, ret_device[slot]).start()
        when(exists(slot), go)

    def at(u, offset, fn):
        c = (u - offset) // SLOTS
        pl.when(both(u >= offset, both((u - offset) % SLOTS == 0, c < chunks)))(lambda: fn(c))

    def exists_dyn(slot):
        a = slot % 3
        ok = jnp.logical_or(a != 0, has_m)
        ok = both(ok, jnp.logical_or(a != 2, has_p))
        return both(ok, jnp.logical_or(slot // 3 != 2, has_xi))

    def step(u, carry):
        at(u, SEND_OWN, lambda c: send_fwd(c, OWN))

        def relay_1(c):
            relay(c, OTHER_0)
            relay(c, OTHER_M)

        at(u, RELAY_1, relay_1)
        at(u, RELAY_2, lambda c: relay(c, SAME_M))
        at(u, RELAY_3, lambda c: relay(c, OTHER_P))

        for slot in (SAME_P, CROSS_0, CROSS_M, CROSS_P):
            at(u, FIRST + FIRST_ORDER.index(slot),
               lambda c, slot=slot: when(exists(slot), lambda: local_wait(fwd, fwd_r, c, slot)))
        c1 = (u - FIRST) // SLOTS
        b1 = pick(FIRST_ORDER, (u - FIRST) % SLOTS)

        @pl.when(both(both(u >= FIRST, c1 < chunks), exists_dyn(b1)))
        def _():
            first_pass(c1, b1)

        for slot in FIRST_ORDER[1:]:
            at(u, FIRST + FIRST_ORDER.index(slot),
               lambda c, slot=slot: when(exists(slot), lambda: st_copy(c, slot).start()))

        at(u, MERGE, merge)

        for slot in SECOND_ORDER[:-1]:
            at(u, SECOND + SECOND_ORDER.index(slot),
               lambda c, slot=slot: when(exists(slot), lambda: local_wait(bc_in, bc_r, c, slot)))
        c2 = (u - SECOND) // SLOTS
        b2 = pick(SECOND_ORDER, (u - SECOND) % SLOTS)

        @pl.when(both(both(u >= SECOND, c2 < chunks), exists_dyn(b2)))
        def _():
            second_pass(c2, b2)

        for slot in SECOND_ORDER[:4]:
            at(u, SECOND + SECOND_ORDER.index(slot), lambda c, slot=slot: hand_back(c, slot))
        at(u, RET_OTHER_P, lambda c: hand_back(c, OTHER_P))
        at(u, RET_OTHER_M, lambda c: hand_back(c, OTHER_M))
        at(u, RET_SAME_M, lambda c: hand_back(c, SAME_M))
        at(u, RET_OTHER_0, lambda c: hand_back(c, OTHER_0))
        at(u, RET_OWN, lambda c: hand_back(c, OWN))
        return carry

    lax.fori_loop(0, RET_OWN + SLOTS * (chunks - 1) + 1, step, 0)

    out_k[...] = (acc_k[...] * scale).astype(jnp.bfloat16)
    out_v[...] = acc_v[...].astype(jnp.bfloat16)
    stores = []
    for h in range(heads):
        for src, ref in ((out_q, dq_hbm), (out_k, dk_hbm), (out_v, dv_hbm)):
            stores.append(pltpu.make_async_copy(src.at[h], ref.at[:, pl.ds(h * HD, HD)], load_sem.at[len(stores)]))
    for copy in stores:
        copy.start()

    def drain(c, carry):
        for a, b, device, ok in fwd_plan:
            when(ok, lambda a=a, b=b, device=device: fwd_copy(c, a, b, device).wait_send())
        for slot in range(SLOTS):
            if slot != OWN:
                def go(slot=slot):
                    st_copy(c, slot).wait_send()
                    bc_copy(c, slot).wait_send()
                    ret_copy(c, slot, ret_device[slot]).wait_send()
                when(exists(slot), go)
        return carry

    lax.fori_loop(0, chunks, drain, 0)
    for copy in stores:
        copy.wait()


def per_device(times, rows, query, key_tiles, value_tiles, grad_out, neighbours):
    _, _, count, tile, channels = query.shape
    heads = channels // HD
    tokens = count * tile
    per_head = 3
    chunk = tokens // per_head
    chunks = heads * per_head
    entries = neighbours[0, 0]
    listed = jnp.any(entries[:, :, None] == jnp.arange(9 * count, dtype=jnp.int32), axis=1)
    listed = listed.reshape(count, 9, count).astype(jnp.float32)
    place = [3 * (0, 1, -1)[slot // 3] + slot % 3 - 1 for slot in range(SLOTS)]
    even = jnp.stack([listed[:, 4 + p] for p in place])
    odd = jnp.stack([listed[:, 4 - p] for p in place])
    listed = jnp.where(lax.axis_index("tm") % 2 == 0, even, odd)
    mask = jnp.repeat(jnp.swapaxes(listed, 1, 2), tile, axis=2)
    mask = mask.reshape(SLOTS, count, per_head, chunk).transpose(2, 0, 1, 3)
    mask = jnp.pad(mask, ((0, 0), (0, 0), (0, 6), (0, 0)))

    flat = [value.reshape(tokens, channels) for value in (query, key_tiles, value_tiles, grad_out)]
    out = jax.ShapeDtypeStruct((tokens, channels), jnp.bfloat16)
    dma = pltpu.SemaphoreType.DMA
    vmem = pltpu.VMEM
    small = (chunks, SLOTS, 8, chunk)
    grads = pl.pallas_call(
        functools.partial(kernel, times, rows, heads, tile),
        out_shape=(out, out, out),
        in_specs=[pl.BlockSpec(memory_space=pl.ANY)] * 4 + [pl.BlockSpec(memory_space=pltpu.VMEM)],
        out_specs=[pl.BlockSpec(memory_space=pl.ANY)] * 3,
        scratch_shapes=[
            vmem((chunks, SLOTS, 2, chunk, HD), jnp.bfloat16),
            vmem((heads, tokens, HD), jnp.bfloat16),
            vmem((heads, tokens, HD), jnp.bfloat16),
            vmem((heads, HD, tokens), jnp.bfloat16),
            vmem((heads, tokens, HD), jnp.float32),
            vmem((heads, tokens, HD), jnp.float32),
            vmem((2, SLOTS, HD, chunk), jnp.float32),
            vmem((chunks, SLOTS, HD, chunk), jnp.bfloat16),
            vmem((chunks, SLOTS, HD, chunk), jnp.bfloat16),
            vmem(small, jnp.float32),
            vmem(small, jnp.float32),
            vmem(small, jnp.float32),
            vmem(small, jnp.float32),
            vmem((heads, tokens, HD), jnp.bfloat16),
            vmem((heads, tokens, HD), jnp.bfloat16),
            vmem((heads, tokens, HD), jnp.bfloat16),
            dma((2 * chunks + 2 * heads,)),
        ] + [dma((chunks, SLOTS))] * 8,
        compiler_params=pltpu.CompilerParams(
            collective_id=0, has_side_effects=True, vmem_limit_bytes=56 * 1024 * 1024
        ),
    )(flat[0], flat[1], flat[2], flat[3], mask)
    return tuple(grad.reshape(query.shape) for grad in grads)


def solution(mesh):
    spec = P("tm", "row", None, None, "head")
    return jax.shard_map(
        functools.partial(per_device, mesh.shape["tm"], mesh.shape["row"]),
        mesh=mesh,
        in_specs=(spec, spec, spec, spec, P("tm", "row", None, None)),
        out_specs=(spec, spec, spec),
        check_vma=False,
    )
```

```python
import functools

import jax
import jax.numpy as jnp
from jax import lax
from jax.experimental import pallas as pl
from jax.experimental.pallas import tpu as pltpu
from jax.sharding import PartitionSpec as P

HD = 128
SLOTS = 9
UNUSED = 1e30
SAME_M, OWN, SAME_P, OTHER_M, OTHER_0, OTHER_P, CROSS_M, CROSS_0, CROSS_P = range(9)
FIRST_ORDER = (OWN, OTHER_0, OTHER_M, SAME_M, SAME_P, OTHER_P, CROSS_0, CROSS_M, CROSS_P)
SECOND_ORDER = (CROSS_P, CROSS_M, CROSS_0, SAME_P, OTHER_P, SAME_M, OTHER_M, OTHER_0, OWN)
SEND_OWN, RELAY_1, RELAY_2, RELAY_3 = 0, 6, 12, 18
FIRST = 22
MERGE = FIRST + 14
SECOND = FIRST + 20
RET_OTHER_P = SECOND + 7
RET_OTHER_M = SECOND + 10
RET_SAME_M = SECOND + 12
RET_OTHER_0 = SECOND + 18
RET_OWN = SECOND + 24
TAKE_MARKS = 2
MESH = pl.DeviceIdType.MESH


def mirror(slot):
    if isinstance(slot, int):
        return 2 - slot if slot < 3 else slot
    return jnp.where(slot < 3, 2 - slot, slot)


def pick(table, index):
    value = jnp.int32(table[0])
    for k in range(1, len(table)):
        value = jnp.where(index == k, jnp.int32(table[k]), value)
    return value


def dot(a, b, dims):
    return lax.dot_general(a, b, (dims, ((), ())), preferred_element_type=jnp.float32)


def kernel(times, rows, heads, tile, q_hbm, k_hbm, v_hbm, g_hbm, mark_out, dq_hbm, dk_hbm, dv_hbm,
           fwd, keys, vals, keys_t, acc_k, acc_v, part, ret_out, ret_in, st_out, st_in, bc_out, bc_in,
           out_q, out_k, out_v, load_sem, fwd_s, fwd_r, st_s, st_r, bc_s, bc_r, ret_s, ret_r, low_p, low_ds, mark_in, marks, mark_s, mark_r):
    chunk = fwd.shape[3]
    per_head = 2 * tile // chunk
    chunks = heads * per_head
    scale = HD ** -0.5
    scale2 = scale * 1.4426950408889634

    t, r = lax.axis_index("tm"), lax.axis_index("row")
    s = 1 - 2 * (t % 2)
    has_m = jnp.logical_and(r - s >= 0, r - s < rows)
    has_p = jnp.logical_and(r + s >= 0, r + s < rows)
    has_xo = jnp.logical_and(t + 2 * s >= 0, t + 2 * s < times)
    has_xi = jnp.logical_and(t - 2 * s >= 0, t - 2 * s < times)
    pair = {"tm": t + s, "row": r}
    outer = {"tm": t + s, "row": r - s}
    x_out = {"tm": t + 2 * s, "row": r}
    x_in = {"tm": t - 2 * s, "row": r}

    def both(a, b):
        return jnp.logical_and(a, b)

    row_ok = (has_m, True, has_p)

    def exists(slot):
        ok = row_ok[slot % 3]
        if slot // 3 == 2:
            ok = has_xi if ok is True else both(ok, has_xi)
        return ok

    def sent_to(slot):
        kind = (slot // 3 + 1) % 3 - 1
        return {"tm": t + s * kind, "row": r + s * (slot % 3 - 1)}

    def when(cond, fn):
        if cond is True:
            fn()
        else:
            pl.when(cond)(fn)

    loads = []
    for c in range(chunks):
        h, k = c // per_head, c % per_head
        for n, ref in enumerate((q_hbm, g_hbm)):
            loads.append(pltpu.make_async_copy(
                ref.at[pl.ds(k * chunk, chunk), pl.ds(h * HD, HD)], fwd.at[c, OWN, n], load_sem.at[len(loads)]))
    for h in range(heads):
        for ref, dst in ((k_hbm, keys), (v_hbm, vals)):
            loads.append(pltpu.make_async_copy(ref.at[:, pl.ds(h * HD, HD)], dst.at[h], load_sem.at[len(loads)]))
    for copy in loads:
        copy.start()

    barrier = pltpu.get_barrier_semaphore()
    greeted = [(sent_to(b), exists(b)) for b in range(SLOTS) if b != OWN] + [(x_out, has_xo), (x_in, has_xi)]
    count = jnp.int32(0)
    for device, ok in greeted:
        def greet(device=device):
            pl.semaphore_signal(barrier, inc=1, device_id=device, device_id_type=MESH)
        when(ok, greet)
        count = count + (1 if ok is True else ok.astype(jnp.int32))
    for copy in loads:
        copy.wait()
    for h in range(heads):
        keys_t[h] = keys[h].T
    acc_k[...] = jnp.zeros_like(acc_k)
    acc_v[...] = jnp.zeros_like(acc_v)
    pl.semaphore_wait(barrier, count)

    def fwd_copy(c, src, dst, device):
        return pltpu.make_async_remote_copy(
            src_ref=fwd.at[c, src], dst_ref=fwd.at[c, dst], send_sem=fwd_s.at[c, dst], recv_sem=fwd_r.at[c, dst],
            device_id=device, device_id_type=MESH)

    def st_copy(c, slot):
        return pltpu.make_async_remote_copy(
            src_ref=st_out.at[c, slot], dst_ref=st_in.at[c, mirror(slot)], send_sem=st_s.at[c, slot],
            recv_sem=st_r.at[c, mirror(slot)], device_id=sent_to(slot), device_id_type=MESH)

    def bc_copy(c, slot):
        return pltpu.make_async_remote_copy(
            src_ref=bc_out.at[c, 0], dst_ref=bc_in.at[c, mirror(slot)], send_sem=bc_s.at[c, slot],
            recv_sem=bc_r.at[c, mirror(slot)], device_id=sent_to(slot), device_id_type=MESH)

    def ret_copy(c, slot, device):
        return pltpu.make_async_remote_copy(
            src_ref=ret_out.at[c, slot], dst_ref=ret_in.at[c, slot], send_sem=ret_s.at[c, slot],
            recv_sem=ret_r.at[c, slot], device_id=device, device_id_type=MESH)

    def local_wait(buf, sems, c, slot):
        pltpu.make_async_copy(buf.at[c, slot], buf.at[c, slot], sems.at[c, slot]).wait()

    def mark_copy(slot):
        return pltpu.make_async_remote_copy(
            src_ref=mark_out.at[slot], dst_ref=mark_in.at[mirror(slot)], send_sem=mark_s.at[slot],
            recv_sem=mark_r.at[mirror(slot)], device_id=sent_to(slot), device_id_type=MESH)

    def take_marks(c):
        for slot in range(SLOTS):
            if slot != OWN:
                when(exists(slot), lambda slot=slot: pltpu.make_async_copy(
                    mark_in.at[slot], mark_in.at[slot], mark_r.at[slot]).wait())
        half = chunk // 2
        for slot in range(SLOTS):
            ref = mark_out if slot == OWN else mark_in
            for k in range(per_head):
                for n in range(2):
                    i = (2 * k + n) // per_head
                    marks[k, slot, :, pl.ds(n * half, half)] = ref[slot, pl.ds(2 * i, 2), :]

    fwd_plan = (
        (OWN, OTHER_0, pair, True), (OWN, OTHER_M, outer, has_m),
        (OTHER_0, SAME_M, outer, has_m), (OTHER_0, CROSS_0, x_out, has_xo),
        (OTHER_M, SAME_P, pair, has_m), (OTHER_M, CROSS_M, x_out, both(has_m, has_xo)),
        (SAME_M, OTHER_P, pair, has_m), (OTHER_P, CROSS_P, x_out, both(has_p, has_xo)),
    )
    ret_device = {
        CROSS_P: x_in, CROSS_M: x_in, CROSS_0: x_in, SAME_P: pair, OTHER_P: pair,
        SAME_M: outer, OTHER_M: outer, OTHER_0: pair,
    }
    ret_adds = {
        OTHER_P: ((CROSS_P, has_xo),), SAME_M: ((OTHER_P, True),), OTHER_M: ((CROSS_M, has_xo), (SAME_P, True)),
        OTHER_0: ((CROSS_0, has_xo), (SAME_M, has_m)), OWN: ((OTHER_M, has_m), (OTHER_0, True)),
    }

    def send_fwd(c, src):
        for a, b, device, ok in fwd_plan:
            if a == src:
                when(ok, lambda a=a, b=b, device=device: fwd_copy(c, a, b, device).start())

    def relay(c, src):
        def go():
            local_wait(fwd, fwd_r, c, src)
            send_fwd(c, src)
        when(exists(src), go)

    def first_pass(c, slot):
        h = c // per_head
        q = fwd[c, slot, 0]
        g = fwd[c, slot, 1]
        parts = []
        for j in range(2):
            used = marks[c % per_head, slot, pl.ds(j, 1), :] > 0.5
            for i in range(3):
                span = pl.ds(j * tile + i * (tile // 3), tile // 3)
                sc = dot(keys[h, span, :], q, ((1,), (1,)))
                peak = jnp.max(sc, axis=0, keepdims=True) * scale2
                e = jnp.exp2(sc * scale2 - peak)
                dp = dot(vals[h, span, :], g, ((1,), (1,)))
                parts.append((used, jnp.where(used, peak, -UNUSED), jnp.sum(e, axis=0, keepdims=True),
                              jnp.sum(e * dp, axis=0, keepdims=True)))
        top = functools.reduce(jnp.maximum, [peak for _, peak, _, _ in parts])
        ws = [jnp.where(used, jnp.exp2(peak - top), 0.0) for used, peak, _, _ in parts]
        total = sum(w * item[2] for w, item in zip(ws, parts))
        mean = sum(w * item[3] for w, item in zip(ws, parts))
        some = jnp.logical_or(parts[0][0], parts[3][0])
        total = jnp.where(some, total, 1.0)
        st_out[c, slot, pl.ds(0, 1), :] = jnp.where(some, top + jnp.log2(total), -UNUSED)
        st_out[c, slot, pl.ds(1, 1), :] = jnp.where(some, mean / total, 0.0)

    def merge(c):
        for slot in range(SLOTS):
            if slot != OWN:
                when(exists(slot), lambda slot=slot: local_wait(st_in, st_r, c, slot))
        lses, means = [], []
        for slot in range(SLOTS):
            ref = st_out if slot == OWN else st_in
            lse, mean = ref[c, slot, pl.ds(0, 1), :], ref[c, slot, pl.ds(1, 1), :]
            ok = exists(slot)
            lses.append(lse if ok is True else jnp.where(ok, lse, -UNUSED))
            means.append(mean if ok is True else jnp.where(ok, mean, 0.0))
        top = functools.reduce(jnp.maximum, lses)
        ws = [jnp.exp2(lse - top) for lse in lses]
        total = sum(ws)
        lse = top + jnp.log2(total)
        delta = sum(w * mean for w, mean in zip(ws, means)) / total
        for ref, slot in ((bc_out, 0), (bc_in, OWN)):
            ref[c, slot, pl.ds(0, 1), :] = lse
            ref[c, slot, pl.ds(1, 1), :] = delta
        for slot in range(SLOTS):
            if slot != OWN:
                when(exists(slot), lambda slot=slot: bc_copy(c, slot).start())

    def second_pass(c, slot):
        h = c // per_head
        q = fwd[c, slot, 0]
        g = fwd[c, slot, 1]
        lse = bc_in[c, slot, pl.ds(0, 1), :]
        delta = bc_in[c, slot, pl.ds(1, 1), :]
        sc = dot(keys[h], q, ((1,), (1,)))
        dp = dot(vals[h], g, ((1,), (1,)))
        for j in range(2):
            span = slice(j * tile, (j + 1) * tile)
            used = marks[c % per_head, slot, pl.ds(j, 1), :] > 0.5
            p = jnp.exp2(sc[span] * scale2 - jnp.where(used, lse, UNUSED))
            low_p[pl.ds(j * tile, tile), :] = p.astype(jnp.bfloat16)
            low_ds[pl.ds(j * tile, tile), :] = (p * (dp[span] - delta)).astype(jnp.bfloat16)
        acc_v[h] += dot(low_p[...], g, ((1,), (0,)))
        acc_k[h] += dot(low_ds[...], q, ((1,), (0,)))
        return dot(keys_t[h], low_ds[...], ((1,), (0,)))

    def hand_back(c, slot):
        def go():
            for src, ok in ret_adds.get(slot, ()):
                def add(src=src):
                    local_wait(ret_in, ret_r, c, src)
                    part[c % 2, slot] += ret_in[c, src].astype(jnp.float32)
                when(ok, add)
            if slot == OWN:
                rows_at = pl.multiple_of((c % per_head) * chunk, chunk)
                out_q[c // per_head, pl.ds(rows_at, chunk), :] = (part[c % 2, slot] * scale).T.astype(jnp.bfloat16)
            else:
                ret_out[c, slot] = part[c % 2, slot].astype(jnp.bfloat16)
                ret_copy(c, slot, ret_device[slot]).start()
        when(exists(slot), go)

    def exists_dyn(slot):
        a = slot % 3
        ok = jnp.logical_or(a != 0, has_m)
        ok = both(ok, jnp.logical_or(a != 2, has_p))
        return both(ok, jnp.logical_or(slot // 3 != 2, has_xi))

    def relay_1(c):
        relay(c, OTHER_0)
        relay(c, OTHER_M)

    events = (
        (SEND_OWN, lambda c: send_fwd(c, OWN)), (RELAY_1, relay_1), (RELAY_2, lambda c: relay(c, SAME_M)),
        (RELAY_3, lambda c: relay(c, OTHER_P)), (MERGE, merge),
        (RET_OTHER_P, lambda c: hand_back(c, OTHER_P)), (RET_OTHER_M, lambda c: hand_back(c, OTHER_M)),
        (RET_SAME_M, lambda c: hand_back(c, SAME_M)), (RET_OTHER_0, lambda c: hand_back(c, OTHER_0)),
        (RET_OWN, lambda c: hand_back(c, OWN)),
    )

    def place(it, b, offset):
        late = b < offset % SLOTS
        c = it - offset // SLOTS - late.astype(jnp.int32)
        index = b - offset % SLOTS + jnp.where(late, SLOTS, 0)
        return c, index, both(c >= 0, c < chunks)

    for slot in range(SLOTS):
        if slot != OWN:
            when(exists(slot), lambda slot=slot: mark_copy(slot).start())

    def step(it, b):
        for k in range(SLOTS):
            here = [(offset // SLOTS, fn) for offset, fn in events if offset % SLOTS == k]

            def run(here=here):
                for lag, fn in here:
                    c = it - lag
                    pl.when(both(c >= 0, c < chunks))(lambda fn=fn, c=c: fn(c))

            if here:
                pl.when(b == k)(run)

        @pl.when(both(it == TAKE_MARKS // SLOTS, b == TAKE_MARKS % SLOTS))
        def _():
            take_marks(0)

        c1, i1, ok1 = place(it, b, FIRST)
        b1 = pick(FIRST_ORDER, i1)

        @pl.when(both(ok1, exists_dyn(b1)))
        def _():
            @pl.when(jnp.logical_or(i1 == FIRST_ORDER.index(SAME_P), i1 >= FIRST_ORDER.index(CROSS_0)))
            def _():
                local_wait(fwd, fwd_r, c1, b1)

            first_pass(c1, b1)

            @pl.when(b1 != OWN)
            def _():
                st_copy(c1, b1).start()

        c2, i2, ok2 = place(it, b, SECOND)
        b2 = pick(SECOND_ORDER, i2)

        @pl.when(both(ok2, exists_dyn(b2)))
        def _():
            @pl.when(b2 != OWN)
            def _():
                local_wait(bc_in, bc_r, c2, b2)

            term = second_pass(c2, b2)

            @pl.when(i2 >= 4)
            def _():
                part[c2 % 2, b2] = term

            @pl.when(i2 < 4)
            def _():
                ret_out[c2, b2] = term.astype(jnp.bfloat16)
                ret_copy(c2, b2, {"tm": jnp.where(i2 == 3, t + s, t - 2 * s), "row": r}).start()

    def chunk_steps(it, carry):
        def one(b, carry):
            step(it, b)
            return carry
        return lax.fori_loop(0, SLOTS, one, carry)

    lax.fori_loop(0, chunks + RET_OWN // SLOTS, chunk_steps, 0)

    out_k[...] = (acc_k[...] * scale).astype(jnp.bfloat16)
    out_v[...] = acc_v[...].astype(jnp.bfloat16)
    stores = []
    for h in range(heads):
        for src, ref in ((out_q, dq_hbm), (out_k, dk_hbm), (out_v, dv_hbm)):
            stores.append(pltpu.make_async_copy(src.at[h], ref.at[:, pl.ds(h * HD, HD)], load_sem.at[len(stores)]))
    for copy in stores:
        copy.start()

    def drain(c, carry):
        for a, b, device, ok in fwd_plan:
            when(ok, lambda a=a, b=b, device=device: fwd_copy(c, a, b, device).wait_send())
        for slot in range(SLOTS):
            if slot != OWN:
                def go(slot=slot):
                    st_copy(c, slot).wait_send()
                    bc_copy(c, slot).wait_send()
                    ret_copy(c, slot, ret_device[slot]).wait_send()
                when(exists(slot), go)
        return carry

    lax.fori_loop(0, chunks, drain, 0)
    for slot in range(SLOTS):
        if slot != OWN:
            when(exists(slot), lambda slot=slot: mark_copy(slot).wait_send())
    for copy in stores:
        copy.wait()


def per_device(times, rows, query, key_tiles, value_tiles, grad_out, neighbours):
    _, _, count, tile, channels = query.shape
    heads = channels // HD
    tokens = count * tile
    per_head = 3
    chunk = tokens // per_head
    chunks = heads * per_head
    entries = neighbours[0, 0]
    place = jnp.array([3 * ((slot // 3 + 1) % 3 - 1) + slot % 3 - 1 for slot in range(SLOTS)], jnp.int32)
    code = 4 + place * (1 - 2 * (lax.axis_index("tm") % 2))
    names = code[:, None] * count + jnp.arange(count * count, dtype=jnp.int32) % count
    listed = jnp.any(names[:, :, None] == jnp.repeat(entries, count, axis=0)[None], axis=2)
    marks = jnp.broadcast_to(listed.astype(jnp.float32)[:, :, None], (SLOTS, count * count, chunk // 2))

    flat = [value.reshape(tokens, channels) for value in (query, key_tiles, value_tiles, grad_out)]
    out = jax.ShapeDtypeStruct((tokens, channels), jnp.bfloat16)
    dma = pltpu.SemaphoreType.DMA
    vmem = pltpu.VMEM
    small = (chunks, SLOTS, 2, chunk)
    grads = pl.pallas_call(
        functools.partial(kernel, times, rows, heads, tile),
        out_shape=(out, out, out),
        in_specs=[pl.BlockSpec(memory_space=pl.ANY)] * 4 + [pl.BlockSpec(memory_space=pltpu.VMEM)],
        out_specs=[pl.BlockSpec(memory_space=pl.ANY)] * 3,
        scratch_shapes=[
            vmem((chunks, SLOTS, 2, chunk, HD), jnp.bfloat16),
            vmem((heads, tokens, HD), jnp.bfloat16),
            vmem((heads, tokens, HD), jnp.bfloat16),
            vmem((heads, HD, tokens), jnp.bfloat16),
            vmem((heads, tokens, HD), jnp.float32),
            vmem((heads, tokens, HD), jnp.float32),
            vmem((2, SLOTS, HD, chunk), jnp.float32),
            vmem((chunks, SLOTS, HD, chunk), jnp.bfloat16),
            vmem((chunks, SLOTS, HD, chunk), jnp.bfloat16),
            vmem(small, jnp.float32),
            vmem(small, jnp.float32),
            vmem((chunks, 1, 2, chunk), jnp.float32),
            vmem(small, jnp.float32),
            vmem((heads, tokens, HD), jnp.bfloat16),
            vmem((heads, tokens, HD), jnp.bfloat16),
            vmem((heads, tokens, HD), jnp.bfloat16),
            dma((2 * chunks + 2 * heads,)),
        ] + [dma((chunks, SLOTS))] * 8 + [vmem((tokens, chunk), jnp.bfloat16)] * 2 + [
            vmem((SLOTS, count * count, chunk // 2), jnp.float32),
            vmem((per_head, SLOTS, 2, chunk), jnp.float32),
            dma((SLOTS,)),
            dma((SLOTS,)),
        ],
        compiler_params=pltpu.CompilerParams(
            collective_id=0, has_side_effects=True, vmem_limit_bytes=56 * 1024 * 1024
        ),
    )(flat[0], flat[1], flat[2], flat[3], marks)
    return tuple(grad.reshape(query.shape) for grad in grads)


def solution(mesh):
    spec = P("tm", "row", None, None, "head")
    return jax.shard_map(
        functools.partial(per_device, mesh.shape["tm"], mesh.shape["row"]),
        mesh=mesh,
        in_specs=(spec, spec, spec, spec, P("tm", "row", None, None)),
        out_specs=(spec, spec, spec),
        check_vma=False,
    )
```

```python
import functools

import jax
import jax.numpy as jnp
from jax import lax
from jax.experimental import pallas as pl
from jax.experimental.pallas import tpu as pltpu
from jax.sharding import PartitionSpec as P

HD = 128
SLOTS = 9
UNUSED = 1e30
SAME_M, OWN, SAME_P, OTHER_M, OTHER_0, OTHER_P, CROSS_M, CROSS_0, CROSS_P = range(9)
FIRST_ORDER = (OTHER_0, OTHER_M, SAME_M, SAME_P, OTHER_P, CROSS_0, CROSS_M, CROSS_P, OWN)
SECOND_ORDER = (OWN, CROSS_P, CROSS_M, CROSS_0, SAME_P, OTHER_P, SAME_M, OTHER_M, OTHER_0)
SEND_OWN, RELAY_1, RELAY_2, RELAY_3 = 0, 6, 12, 18
FIRST = 15
MERGE = FIRST + 16
SECOND = FIRST + 22
RET_OTHER_P = SECOND + 8
RET_OTHER_M = SECOND + 11
RET_SAME_M = SECOND + 13
RET_OTHER_0 = SECOND + 19
RET_OWN = SECOND + 25
STORE_KV = SECOND + 9
DRAIN = RET_OWN + 1
SET_UP = 2
MESH = pl.DeviceIdType.MESH


def mirror(slot):
    if isinstance(slot, int):
        return 2 - slot if slot < 3 else slot
    return jnp.where(slot < 3, 2 - slot, slot)


def pick(table, index):
    value = jnp.int32(table[0])
    for k in range(1, len(table)):
        value = jnp.where(index == k, jnp.int32(table[k]), value)
    return value


def dot(a, b, dims):
    return lax.dot_general(a, b, (dims, ((), ())), preferred_element_type=jnp.float32)


def kernel(times, rows, heads, tile, q_hbm, k_hbm, v_hbm, g_hbm, mark_out, dq_hbm, dk_hbm, dv_hbm,
           fwd, keys, vals, keys_t, acc_k, acc_v, part, ret_out, ret_in, st_out, st_in, bc_out, bc_in,
           out_q, out_k, out_v, load_sem, fwd_s, fwd_r, st_s, st_r, bc_s, bc_r, ret_s, ret_r, low_p, low_ds, mark_in, marks, mark_s, mark_r, store_sem):
    chunk = fwd.shape[3]
    per_head = 2 * tile // chunk
    chunks = heads * per_head
    scale = HD ** -0.5
    scale2 = scale * 1.4426950408889634

    t, r = lax.axis_index("tm"), lax.axis_index("row")
    s = 1 - 2 * (t % 2)
    has_m = jnp.logical_and(r - s >= 0, r - s < rows)
    has_p = jnp.logical_and(r + s >= 0, r + s < rows)
    has_xo = jnp.logical_and(t + 2 * s >= 0, t + 2 * s < times)
    has_xi = jnp.logical_and(t - 2 * s >= 0, t - 2 * s < times)
    pair = {"tm": t + s, "row": r}
    outer = {"tm": t + s, "row": r - s}
    x_out = {"tm": t + 2 * s, "row": r}
    x_in = {"tm": t - 2 * s, "row": r}

    def both(a, b):
        return jnp.logical_and(a, b)

    row_ok = (has_m, True, has_p)

    def exists(slot):
        ok = row_ok[slot % 3]
        if slot // 3 == 2:
            ok = has_xi if ok is True else both(ok, has_xi)
        return ok

    def sent_to(slot):
        kind = (slot // 3 + 1) % 3 - 1
        return {"tm": t + s * kind, "row": r + s * (slot % 3 - 1)}

    def when(cond, fn):
        if cond is True:
            fn()
        else:
            pl.when(cond)(fn)

    loads = []
    for c in range(chunks):
        h, k = c // per_head, c % per_head
        for n, ref in enumerate((q_hbm, g_hbm)):
            loads.append(pltpu.make_async_copy(
                ref.at[pl.ds(k * chunk, chunk), pl.ds(h * HD, HD)], fwd.at[c, OWN, n], load_sem.at[len(loads)]))
    for h in range(heads):
        for ref, dst in ((k_hbm, keys), (v_hbm, vals)):
            loads.append(pltpu.make_async_copy(ref.at[:, pl.ds(h * HD, HD)], dst.at[h], load_sem.at[len(loads)]))
    for copy in loads:
        copy.start()

    barrier = pltpu.get_barrier_semaphore()
    greeted = [(sent_to(b), exists(b)) for b in range(SLOTS) if b != OWN] + [(x_out, has_xo), (x_in, has_xi)]
    count = jnp.int32(0)
    for device, ok in greeted:
        def greet(device=device):
            pl.semaphore_signal(barrier, inc=1, device_id=device, device_id_type=MESH)
        when(ok, greet)
        count = count + (1 if ok is True else ok.astype(jnp.int32))
    pl.semaphore_wait(barrier, count)

    def fwd_copy(c, src, dst, device):
        return pltpu.make_async_remote_copy(
            src_ref=fwd.at[c, src], dst_ref=fwd.at[c, dst], send_sem=fwd_s.at[c, dst], recv_sem=fwd_r.at[c, dst],
            device_id=device, device_id_type=MESH)

    def st_copy(c, slot):
        return pltpu.make_async_remote_copy(
            src_ref=st_out.at[c, slot], dst_ref=st_in.at[c, mirror(slot)], send_sem=st_s.at[c, slot],
            recv_sem=st_r.at[c, mirror(slot)], device_id=sent_to(slot), device_id_type=MESH)

    def bc_copy(c, slot):
        return pltpu.make_async_remote_copy(
            src_ref=bc_out.at[c, 0], dst_ref=bc_in.at[c, mirror(slot)], send_sem=bc_s.at[c, slot],
            recv_sem=bc_r.at[c, mirror(slot)], device_id=sent_to(slot), device_id_type=MESH)

    def ret_copy(c, slot, device):
        return pltpu.make_async_remote_copy(
            src_ref=ret_out.at[c, slot], dst_ref=ret_in.at[c, slot], send_sem=ret_s.at[c, slot],
            recv_sem=ret_r.at[c, slot], device_id=device, device_id_type=MESH)

    def local_wait(buf, sems, c, slot):
        pltpu.make_async_copy(buf.at[c, slot], buf.at[c, slot], sems.at[c, slot]).wait()

    def mark_copy(slot):
        return pltpu.make_async_remote_copy(
            src_ref=mark_out.at[slot], dst_ref=mark_in.at[mirror(slot)], send_sem=mark_s.at[slot],
            recv_sem=mark_r.at[mirror(slot)], device_id=sent_to(slot), device_id_type=MESH)

    def take_marks():
        for slot in range(SLOTS):
            if slot != OWN:
                when(exists(slot), lambda slot=slot: pltpu.make_async_copy(
                    mark_in.at[slot], mark_in.at[slot], mark_r.at[slot]).wait())
        half = chunk // 2
        for slot in range(SLOTS):
            ref = mark_out if slot == OWN else mark_in
            for k in range(per_head):
                for n in range(2):
                    i = (2 * k + n) // per_head
                    marks[k, slot, :, pl.ds(n * half, half)] = ref[slot, pl.ds(2 * i, 2), :]

    fwd_plan = (
        (OWN, OTHER_0, pair, True), (OWN, OTHER_M, outer, has_m),
        (OTHER_0, SAME_M, outer, has_m), (OTHER_0, CROSS_0, x_out, has_xo),
        (OTHER_M, SAME_P, pair, has_m), (OTHER_M, CROSS_M, x_out, both(has_m, has_xo)),
        (SAME_M, OTHER_P, pair, has_m), (OTHER_P, CROSS_P, x_out, both(has_p, has_xo)),
    )
    ret_device = {
        CROSS_P: x_in, CROSS_M: x_in, CROSS_0: x_in, SAME_P: pair, OTHER_P: pair,
        SAME_M: outer, OTHER_M: outer, OTHER_0: pair,
    }
    ret_adds = {
        OTHER_P: ((CROSS_P, has_xo),), SAME_M: ((OTHER_P, True),), OTHER_M: ((CROSS_M, has_xo), (SAME_P, True)),
        OTHER_0: ((CROSS_0, has_xo), (SAME_M, has_m)), OWN: ((OTHER_M, has_m), (OTHER_0, True)),
    }

    def send_fwd(c, src):
        for a, b, device, ok in fwd_plan:
            if a == src:
                when(ok, lambda a=a, b=b, device=device: fwd_copy(c, a, b, device).start())

    def send_own(c):
        for n in range(2):
            pltpu.make_async_copy(fwd.at[c, OWN, n], fwd.at[c, OWN, n], load_sem.at[2 * c + n]).wait()
        send_fwd(c, OWN)

    def relay(c, src):
        def go():
            local_wait(fwd, fwd_r, c, src)
            send_fwd(c, src)
        when(exists(src), go)

    def first_pass(c, slot):
        h = c // per_head
        q = fwd[c, slot, 0]
        g = fwd[c, slot, 1]
        parts = []
        for j in range(2):
            used = marks[c % per_head, slot, pl.ds(j, 1), :] > 0.5
            for i in range(3):
                span = pl.ds(j * tile + i * (tile // 3), tile // 3)
                sc = dot(keys[h, span, :], q, ((1,), (1,)))
                peak = jnp.max(sc, axis=0, keepdims=True) * scale2
                e = jnp.exp2(sc * scale2 - peak)
                dp = dot(vals[h, span, :], g, ((1,), (1,)))
                parts.append((used, jnp.where(used, peak, -UNUSED), jnp.sum(e, axis=0, keepdims=True),
                              jnp.sum(e * dp, axis=0, keepdims=True)))
        top = functools.reduce(jnp.maximum, [peak for _, peak, _, _ in parts])
        ws = [jnp.where(used, jnp.exp2(peak - top), 0.0) for used, peak, _, _ in parts]
        total = sum(w * item[2] for w, item in zip(ws, parts))
        mean = sum(w * item[3] for w, item in zip(ws, parts))
        some = jnp.logical_or(parts[0][0], parts[3][0])
        total = jnp.where(some, total, 1.0)
        st_out[c, slot, pl.ds(0, 1), :] = jnp.where(some, top + jnp.log2(total), -UNUSED)
        st_out[c, slot, pl.ds(1, 1), :] = jnp.where(some, mean / total, 0.0)

    def merge(c):
        for slot in range(SLOTS):
            if slot != OWN:
                when(exists(slot), lambda slot=slot: local_wait(st_in, st_r, c, slot))
        lses, means = [], []
        for slot in range(SLOTS):
            ref = st_out if slot == OWN else st_in
            lse, mean = ref[c, slot, pl.ds(0, 1), :], ref[c, slot, pl.ds(1, 1), :]
            ok = exists(slot)
            lses.append(lse if ok is True else jnp.where(ok, lse, -UNUSED))
            means.append(mean if ok is True else jnp.where(ok, mean, 0.0))
        top = functools.reduce(jnp.maximum, lses)
        ws = [jnp.exp2(lse - top) for lse in lses]
        total = sum(ws)
        lse = top + jnp.log2(total)
        delta = sum(w * mean for w, mean in zip(ws, means)) / total
        for ref, slot in ((bc_out, 0), (bc_in, OWN)):
            ref[c, slot, pl.ds(0, 1), :] = lse
            ref[c, slot, pl.ds(1, 1), :] = delta
        for slot in range(SLOTS):
            if slot != OWN:
                when(exists(slot), lambda slot=slot: bc_copy(c, slot).start())

    def second_pass(c, slot):
        h = c // per_head
        q = fwd[c, slot, 0]
        g = fwd[c, slot, 1]
        lse = bc_in[c, slot, pl.ds(0, 1), :]
        delta = bc_in[c, slot, pl.ds(1, 1), :]
        sc = dot(keys[h], q, ((1,), (1,)))
        dp = dot(vals[h], g, ((1,), (1,)))
        for j in range(2):
            span = slice(j * tile, (j + 1) * tile)
            used = marks[c % per_head, slot, pl.ds(j, 1), :] > 0.5
            p = jnp.exp2(sc[span] * scale2 - jnp.where(used, lse, UNUSED))
            low_p[pl.ds(j * tile, tile), :] = p.astype(jnp.bfloat16)
            low_ds[pl.ds(j * tile, tile), :] = (p * (dp[span] - delta)).astype(jnp.bfloat16)
        acc_v[h] += dot(low_p[...], g, ((1,), (0,)))
        acc_k[h] += dot(low_ds[...], q, ((1,), (0,)))
        dq_t = dot(keys_t[h], low_ds[...], ((1,), (0,)))
        part[c % 4, slot] = dq_t
        ret_out[c, slot] = dq_t.astype(jnp.bfloat16)

    def store(h, n):
        src, ref = ((out_q, dq_hbm), (out_k, dk_hbm), (out_v, dv_hbm))[n]
        columns = pl.ds(h * HD if isinstance(h, int) else pl.multiple_of(h * HD, HD), HD)
        return pltpu.make_async_copy(src.at[h], ref.at[:, columns], store_sem.at[h, n])

    def store_kv(c):
        @pl.when(c % per_head == per_head - 1)
        def _():
            h = c // per_head
            out_k[h] = (acc_k[h] * scale).astype(jnp.bfloat16)
            out_v[h] = acc_v[h].astype(jnp.bfloat16)
            store(h, 1).start()
            store(h, 2).start()

    def drain(c):
        for a, b, device, ok in fwd_plan:
            when(ok, lambda a=a, b=b, device=device: fwd_copy(c, a, b, device).wait_send())
        for slot in range(SLOTS):
            if slot != OWN:
                def go(slot=slot):
                    st_copy(c, slot).wait_send()
                    bc_copy(c, slot).wait_send()
                    ret_copy(c, slot, ret_device[slot]).wait_send()
                when(exists(slot), go)

    def hand_back(c, slot):
        def go():
            for src, ok in ret_adds.get(slot, ()):
                def add(src=src):
                    local_wait(ret_in, ret_r, c, src)
                    part[c % 4, slot] += ret_in[c, src].astype(jnp.float32)
                when(ok, add)
            if slot == OWN:
                rows_at = pl.multiple_of((c % per_head) * chunk, chunk)
                out_q[c // per_head, pl.ds(rows_at, chunk), :] = (part[c % 4, slot] * scale).T.astype(jnp.bfloat16)

                @pl.when(c % per_head == per_head - 1)
                def _():
                    store(c // per_head, 0).start()
            else:
                ret_out[c, slot] = part[c % 4, slot].astype(jnp.bfloat16)
                ret_copy(c, slot, ret_device[slot]).start()
        when(exists(slot), go)

    def exists_dyn(slot):
        a = slot % 3
        ok = jnp.logical_or(a != 0, has_m)
        ok = both(ok, jnp.logical_or(a != 2, has_p))
        return both(ok, jnp.logical_or(slot // 3 != 2, has_xi))

    def relay_1(c):
        relay(c, OTHER_0)
        relay(c, OTHER_M)

    events = (
        (SEND_OWN, send_own), (RELAY_1, relay_1), (RELAY_2, lambda c: relay(c, SAME_M)),
        (RELAY_3, lambda c: relay(c, OTHER_P)), (MERGE, merge),
        (RET_OTHER_P, lambda c: hand_back(c, OTHER_P)), (RET_OTHER_M, lambda c: hand_back(c, OTHER_M)),
        (RET_SAME_M, lambda c: hand_back(c, SAME_M)), (RET_OTHER_0, lambda c: hand_back(c, OTHER_0)),
        (RET_OWN, lambda c: hand_back(c, OWN)), (STORE_KV, store_kv), (DRAIN, drain),
    )

    def place(it, b, offset):
        late = b < offset % SLOTS
        c = it - offset // SLOTS - late.astype(jnp.int32)
        index = b - offset % SLOTS + jnp.where(late, SLOTS, 0)
        return c, index, both(c >= 0, c < chunks)

    for slot in range(SLOTS):
        if slot != OWN:
            when(exists(slot), lambda slot=slot: mark_copy(slot).start())

    def step(it, b):
        for k in range(SLOTS):
            here = [(offset // SLOTS, fn) for offset, fn in events if offset % SLOTS == k]

            def run(here=here):
                for lag, fn in here:
                    c = it - lag
                    pl.when(both(c >= 0, c < chunks))(lambda fn=fn, c=c: fn(c))

            if here:
                pl.when(b == k)(run)

        @pl.when(both(it == SET_UP // SLOTS, b == SET_UP % SLOTS))
        def _():
            for copy in loads[2 * chunks:]:
                copy.wait()
            for h in range(heads):
                keys_t[h] = keys[h].T
            acc_k[...] = jnp.zeros_like(acc_k)
            acc_v[...] = jnp.zeros_like(acc_v)
            take_marks()

        c1, i1, ok1 = place(it, b, FIRST)
        b1 = pick(FIRST_ORDER, i1)

        @pl.when(both(ok1, exists_dyn(b1)))
        def _():
            @pl.when(jnp.logical_or(b1 == SAME_P, b1 >= CROSS_M))
            def _():
                local_wait(fwd, fwd_r, c1, b1)

            first_pass(c1, b1)

            @pl.when(b1 != OWN)
            def _():
                st_copy(c1, b1).start()

        c2, i2, ok2 = place(it, b, SECOND)
        b2 = pick(SECOND_ORDER, i2)

        @pl.when(both(ok2, exists_dyn(b2)))
        def _():
            @pl.when(b2 != OWN)
            def _():
                local_wait(bc_in, bc_r, c2, b2)

            second_pass(c2, b2)

            @pl.when(jnp.logical_or(b2 == SAME_P, b2 >= CROSS_M))
            def _():
                ret_copy(c2, b2, {"tm": jnp.where(b2 == SAME_P, t + s, t - 2 * s), "row": r}).start()

    def chunk_steps(it, carry):
        def one(b, carry):
            step(it, b)
            return carry
        return lax.fori_loop(0, SLOTS, one, carry)

    lax.fori_loop(0, chunks + DRAIN // SLOTS, chunk_steps, 0)

    for slot in range(SLOTS):
        if slot != OWN:
            when(exists(slot), lambda slot=slot: mark_copy(slot).wait_send())
    for h in range(heads):
        for n in range(3):
            store(h, n).wait()


def per_device(times, rows, query, key_tiles, value_tiles, grad_out, neighbours):
    _, _, count, tile, channels = query.shape
    heads = channels // HD
    tokens = count * tile
    per_head = 3
    chunk = tokens // per_head
    chunks = heads * per_head
    entries = neighbours[0, 0]
    slots = jnp.arange(SLOTS, dtype=jnp.int32)
    place = 3 * ((slots // 3 + 1) % 3 - 1) + slots % 3 - 1
    code = 4 + place * (1 - 2 * (lax.axis_index("tm") % 2))
    names = code[:, None] * count + jnp.arange(count * count, dtype=jnp.int32) % count
    listed = jnp.any(names[:, :, None] == jnp.repeat(entries, count, axis=0)[None], axis=2)
    marks = jnp.broadcast_to(listed.astype(jnp.float32)[:, :, None], (SLOTS, count * count, chunk // 2))

    flat = [value.reshape(tokens, channels) for value in (query, key_tiles, value_tiles, grad_out)]
    out = jax.ShapeDtypeStruct((tokens, channels), jnp.bfloat16)
    dma = pltpu.SemaphoreType.DMA
    vmem = pltpu.VMEM
    small = (chunks, SLOTS, 2, chunk)
    grads = pl.pallas_call(
        functools.partial(kernel, times, rows, heads, tile),
        out_shape=(out, out, out),
        in_specs=[pl.BlockSpec(memory_space=pl.ANY)] * 4 + [pl.BlockSpec(memory_space=pltpu.VMEM)],
        out_specs=[pl.BlockSpec(memory_space=pl.ANY)] * 3,
        scratch_shapes=[
            vmem((chunks, SLOTS, 2, chunk, HD), jnp.bfloat16),
            vmem((heads, tokens, HD), jnp.bfloat16),
            vmem((heads, tokens, HD), jnp.bfloat16),
            vmem((heads, HD, tokens), jnp.bfloat16),
            vmem((heads, tokens, HD), jnp.float32),
            vmem((heads, tokens, HD), jnp.float32),
            vmem((4, SLOTS, HD, chunk), jnp.float32),
            vmem((chunks, SLOTS, HD, chunk), jnp.bfloat16),
            vmem((chunks, SLOTS, HD, chunk), jnp.bfloat16),
            vmem(small, jnp.float32),
            vmem(small, jnp.float32),
            vmem((chunks, 1, 2, chunk), jnp.float32),
            vmem(small, jnp.float32),
            vmem((heads, tokens, HD), jnp.bfloat16),
            vmem((heads, tokens, HD), jnp.bfloat16),
            vmem((heads, tokens, HD), jnp.bfloat16),
            dma((2 * chunks + 2 * heads,)),
        ] + [dma((chunks, SLOTS))] * 8 + [vmem((tokens, chunk), jnp.bfloat16)] * 2 + [
            vmem((SLOTS, count * count, chunk // 2), jnp.float32),
            vmem((per_head, SLOTS, 2, chunk), jnp.float32),
            dma((SLOTS,)),
            dma((SLOTS,)),
            dma((heads, 3)),
        ],
        compiler_params=pltpu.CompilerParams(
            collective_id=0, has_side_effects=True, vmem_limit_bytes=56 * 1024 * 1024
        ),
    )(flat[0], flat[1], flat[2], flat[3], marks)
    return tuple(grad.reshape(query.shape) for grad in grads)


def solution(mesh):
    spec = P("tm", "row", None, None, "head")
    return jax.shard_map(
        functools.partial(per_device, mesh.shape["tm"], mesh.shape["row"]),
        mesh=mesh,
        in_specs=(spec, spec, spec, spec, P("tm", "row", None, None)),
        out_specs=(spec, spec, spec),
        check_vma=False,
    )
```

```python
import functools

import jax
import jax.numpy as jnp
from jax import lax
from jax.experimental import pallas as pl
from jax.experimental.pallas import tpu as pltpu
from jax.sharding import PartitionSpec as P

HD = 128
SLOTS = 9
UNUSED = 1e30
SAME_M, OWN, SAME_P, OTHER_M, OTHER_0, OTHER_P, CROSS_M, CROSS_0, CROSS_P = range(9)
FIRST_ORDER = (OTHER_0, OTHER_M, SAME_M, SAME_P, OTHER_P, CROSS_0, CROSS_M, CROSS_P, OWN)
SECOND_ORDER = (OWN, CROSS_P, CROSS_M, CROSS_0, SAME_P, OTHER_P, SAME_M, OTHER_M, OTHER_0)
SEND_OWN, RELAY_1, RELAY_2, RELAY_3 = 0, 6, 12, 18
FIRST = 15
MERGE = FIRST + 16
SECOND = FIRST + 22
RET_OTHER_P = SECOND + 8
RET_OTHER_M = SECOND + 11
RET_SAME_M = SECOND + 13
RET_OTHER_0 = SECOND + 19
RET_OWN = SECOND + 25
STORE_KV = SECOND + 9
DRAIN = RET_OWN + 1
SET_UP = 2
MESH = pl.DeviceIdType.MESH


def mirror(slot):
    if isinstance(slot, int):
        return 2 - slot if slot < 3 else slot
    return jnp.where(slot < 3, 2 - slot, slot)


def pick(table, index):
    value = jnp.int32(table[0])
    for k in range(1, len(table)):
        value = jnp.where(index == k, jnp.int32(table[k]), value)
    return value


def dot(a, b, dims):
    return lax.dot_general(a, b, (dims, ((), ())), preferred_element_type=jnp.float32)


def kernel(times, rows, heads, tile, q_hbm, k_hbm, v_hbm, g_hbm, mark_out, dq_hbm, dk_hbm, dv_hbm,
           fwd, keys, vals, keys_t, acc_k, acc_v, part, ret_out, ret_in, st_out, st_in, bc_out, bc_in,
           out_q, out_k, out_v, load_sem, fwd_s, fwd_r, st_s, st_r, bc_s, bc_r, ret_s, ret_r, low_p, low_ds, mark_in, marks, mark_s, mark_r, store_sem):
    chunk = fwd.shape[3]
    per_head = 2 * tile // chunk
    chunks = heads * per_head
    scale = HD ** -0.5
    scale2 = scale * 1.4426950408889634

    t, r = lax.axis_index("tm"), lax.axis_index("row")
    s = 1 - 2 * (t % 2)
    has_m = jnp.logical_and(r - s >= 0, r - s < rows)
    has_p = jnp.logical_and(r + s >= 0, r + s < rows)
    has_xo = jnp.logical_and(t + 2 * s >= 0, t + 2 * s < times)
    has_xi = jnp.logical_and(t - 2 * s >= 0, t - 2 * s < times)
    pair = {"tm": t + s, "row": r}
    outer = {"tm": t + s, "row": r - s}
    x_out = {"tm": t + 2 * s, "row": r}
    x_in = {"tm": t - 2 * s, "row": r}

    def both(a, b):
        return jnp.logical_and(a, b)

    row_ok = (has_m, True, has_p)

    def exists(slot):
        ok = row_ok[slot % 3]
        if slot // 3 == 2:
            ok = has_xi if ok is True else both(ok, has_xi)
        return ok

    def sent_to(slot):
        kind = (slot // 3 + 1) % 3 - 1
        return {"tm": t + s * kind, "row": r + s * (slot % 3 - 1)}

    def when(cond, fn):
        if cond is True:
            fn()
        else:
            pl.when(cond)(fn)

    loads = []
    for c in range(chunks):
        h, k = c // per_head, c % per_head
        for n, ref in enumerate((q_hbm, g_hbm)):
            loads.append(pltpu.make_async_copy(
                ref.at[pl.ds(k * chunk, chunk), pl.ds(h * HD, HD)], fwd.at[c, OWN, n], load_sem.at[len(loads)]))
    for h in range(heads):
        for ref, dst in ((k_hbm, keys), (v_hbm, vals)):
            loads.append(pltpu.make_async_copy(ref.at[:, pl.ds(h * HD, HD)], dst.at[h], load_sem.at[len(loads)]))
    for copy in loads:
        copy.start()

    barrier = pltpu.get_barrier_semaphore()
    greeted = [(sent_to(b), exists(b)) for b in range(SLOTS) if b != OWN] + [(x_out, has_xo), (x_in, has_xi)]
    count = jnp.int32(0)
    for device, ok in greeted:
        def greet(device=device):
            pl.semaphore_signal(barrier, inc=1, device_id=device, device_id_type=MESH)
        when(ok, greet)
        count = count + (1 if ok is True else ok.astype(jnp.int32))
    pl.semaphore_wait(barrier, count)

    def fwd_copy(c, src, dst, device):
        return pltpu.make_async_remote_copy(
            src_ref=fwd.at[c, src], dst_ref=fwd.at[c, dst], send_sem=fwd_s.at[c, dst], recv_sem=fwd_r.at[c, dst],
            device_id=device, device_id_type=MESH)

    def st_copy(c, slot):
        return pltpu.make_async_remote_copy(
            src_ref=st_out.at[c, slot], dst_ref=st_in.at[c, mirror(slot)], send_sem=st_s.at[c, slot],
            recv_sem=st_r.at[c, mirror(slot)], device_id=sent_to(slot), device_id_type=MESH)

    def bc_copy(c, slot):
        return pltpu.make_async_remote_copy(
            src_ref=bc_out.at[c, 0], dst_ref=bc_in.at[c, mirror(slot)], send_sem=bc_s.at[c, slot],
            recv_sem=bc_r.at[c, mirror(slot)], device_id=sent_to(slot), device_id_type=MESH)

    def ret_copy(c, slot, device):
        return pltpu.make_async_remote_copy(
            src_ref=ret_out.at[c, slot], dst_ref=ret_in.at[c, slot], send_sem=ret_s.at[c, slot],
            recv_sem=ret_r.at[c, slot], device_id=device, device_id_type=MESH)

    def local_wait(buf, sems, c, slot):
        pltpu.make_async_copy(buf.at[c, slot], buf.at[c, slot], sems.at[c, slot]).wait()

    def mark_copy(slot):
        return pltpu.make_async_remote_copy(
            src_ref=mark_out.at[slot], dst_ref=mark_in.at[mirror(slot)], send_sem=mark_s.at[slot],
            recv_sem=mark_r.at[mirror(slot)], device_id=sent_to(slot), device_id_type=MESH)

    def take_marks():
        for slot in range(SLOTS):
            if slot != OWN:
                when(exists(slot), lambda slot=slot: pltpu.make_async_copy(
                    mark_in.at[slot], mark_in.at[slot], mark_r.at[slot]).wait())
        half = chunk // 2
        for slot in range(SLOTS):
            ref = mark_out if slot == OWN else mark_in
            for k in range(per_head):
                for n in range(2):
                    i = (2 * k + n) // per_head
                    marks[k, slot, :, pl.ds(n * half, half)] = ref[slot, pl.ds(2 * i, 2), :]

    fwd_plan = (
        (OWN, OTHER_0, pair, True), (OWN, OTHER_M, outer, has_m),
        (OTHER_0, SAME_M, outer, has_m), (OTHER_0, CROSS_0, x_out, has_xo),
        (OTHER_M, SAME_P, pair, has_m), (OTHER_M, CROSS_M, x_out, both(has_m, has_xo)),
        (SAME_M, OTHER_P, pair, has_m), (OTHER_P, CROSS_P, x_out, both(has_p, has_xo)),
    )
    ret_device = {
        CROSS_P: x_in, CROSS_M: x_in, CROSS_0: x_in, SAME_P: pair, OTHER_P: pair,
        SAME_M: outer, OTHER_M: outer, OTHER_0: pair,
    }
    ret_adds = {
        OTHER_P: ((CROSS_P, has_xo),), SAME_M: ((OTHER_P, True),), OTHER_M: ((CROSS_M, has_xo), (SAME_P, True)),
        OTHER_0: ((CROSS_0, has_xo), (SAME_M, has_m)), OWN: ((OTHER_M, has_m), (OTHER_0, True)),
    }

    def send_fwd(c, src):
        for a, b, device, ok in fwd_plan:
            if a == src:
                when(ok, lambda a=a, b=b, device=device: fwd_copy(c, a, b, device).start())

    def send_own(c):
        for n in range(2):
            pltpu.make_async_copy(fwd.at[c, OWN, n], fwd.at[c, OWN, n], load_sem.at[2 * c + n]).wait()
        send_fwd(c, OWN)

    def relay(c, src):
        def go():
            local_wait(fwd, fwd_r, c, src)
            send_fwd(c, src)
        when(exists(src), go)

    def first_pass(c, slot):
        h = c // per_head
        q = fwd[c, slot, 0]
        g = fwd[c, slot, 1]
        parts = []
        for j in range(2):
            used = marks[c % per_head, slot, pl.ds(j, 1), :] > 0.5
            for i in range(3):
                span = pl.ds(j * tile + i * (tile // 3), tile // 3)
                sc = dot(keys[h, span, :], q, ((1,), (1,)))
                peak = jnp.max(sc, axis=0, keepdims=True) * scale2
                e = jnp.exp2(sc * scale2 - peak)
                dp = dot(vals[h, span, :], g, ((1,), (1,)))
                parts.append((used, jnp.where(used, peak, -UNUSED), jnp.sum(e, axis=0, keepdims=True),
                              jnp.sum(e * dp, axis=0, keepdims=True)))
        top = functools.reduce(jnp.maximum, [peak for _, peak, _, _ in parts])
        ws = [jnp.where(used, jnp.exp2(peak - top), 0.0) for used, peak, _, _ in parts]
        total = sum(w * item[2] for w, item in zip(ws, parts))
        mean = sum(w * item[3] for w, item in zip(ws, parts))
        some = jnp.logical_or(parts[0][0], parts[3][0])
        total = jnp.where(some, total, 1.0)
        st_out[c, slot, pl.ds(0, 1), :] = jnp.where(some, top + jnp.log2(total), -UNUSED)
        st_out[c, slot, pl.ds(1, 1), :] = jnp.where(some, mean / total, 0.0)

    def merge(c):
        for slot in range(SLOTS):
            if slot != OWN:
                when(exists(slot), lambda slot=slot: local_wait(st_in, st_r, c, slot))
        lses, means = [], []
        for slot in range(SLOTS):
            ref = st_out if slot == OWN else st_in
            lse, mean = ref[c, slot, pl.ds(0, 1), :], ref[c, slot, pl.ds(1, 1), :]
            ok = exists(slot)
            lses.append(lse if ok is True else jnp.where(ok, lse, -UNUSED))
            means.append(mean if ok is True else jnp.where(ok, mean, 0.0))
        top = functools.reduce(jnp.maximum, lses)
        ws = [jnp.exp2(lse - top) for lse in lses]
        total = sum(ws)
        lse = top + jnp.log2(total)
        delta = sum(w * mean for w, mean in zip(ws, means)) / total
        for ref, slot in ((bc_out, 0), (bc_in, OWN)):
            ref[c, slot, pl.ds(0, 1), :] = lse
            ref[c, slot, pl.ds(1, 1), :] = delta
        for slot in range(SLOTS):
            if slot != OWN:
                when(exists(slot), lambda slot=slot: bc_copy(c, slot).start())

    def second_pass(c, slot):
        h = c // per_head
        q = fwd[c, slot, 0]
        g = fwd[c, slot, 1]
        lse = bc_in[c, slot, pl.ds(0, 1), :]
        delta = bc_in[c, slot, pl.ds(1, 1), :]
        sc = dot(keys[h], q, ((1,), (1,)))
        dp = dot(vals[h], g, ((1,), (1,)))
        for j in range(2):
            span = slice(j * tile, (j + 1) * tile)
            used = marks[c % per_head, slot, pl.ds(j, 1), :] > 0.5
            p = jnp.exp2(sc[span] * scale2 - jnp.where(used, lse, UNUSED))
            low_p[pl.ds(j * tile, tile), :] = p.astype(jnp.bfloat16)
            low_ds[pl.ds(j * tile, tile), :] = (p * (dp[span] - delta)).astype(jnp.bfloat16)
        acc_v[h] += dot(low_p[...], g, ((1,), (0,)))
        acc_k[h] += dot(low_ds[...], q, ((1,), (0,)))
        dq_t = dot(keys_t[h], low_ds[...], ((1,), (0,)))
        part[c % 4, slot] = dq_t
        ret_out[c, slot] = dq_t.astype(jnp.bfloat16)

    def store(h, n):
        src, ref = ((out_q, dq_hbm), (out_k, dk_hbm), (out_v, dv_hbm))[n]
        columns = pl.ds(h * HD if isinstance(h, int) else pl.multiple_of(h * HD, HD), HD)
        return pltpu.make_async_copy(src.at[h], ref.at[:, columns], store_sem.at[h, n])

    def store_kv(c):
        @pl.when(c % per_head == per_head - 1)
        def _():
            h = c // per_head
            out_k[h] = (acc_k[h] * scale).astype(jnp.bfloat16)
            out_v[h] = acc_v[h].astype(jnp.bfloat16)
            store(h, 1).start()
            store(h, 2).start()

    def drain(c):
        for a, b, device, ok in fwd_plan:
            when(ok, lambda a=a, b=b, device=device: fwd_copy(c, a, b, device).wait_send())
        for slot in range(SLOTS):
            if slot != OWN:
                def go(slot=slot):
                    st_copy(c, slot).wait_send()
                    bc_copy(c, slot).wait_send()
                    ret_copy(c, slot, ret_device[slot]).wait_send()
                when(exists(slot), go)

    def hand_back(c, slot):
        def go():
            for src, ok in ret_adds.get(slot, ()):
                def add(src=src):
                    local_wait(ret_in, ret_r, c, src)
                    part[c % 4, slot] += ret_in[c, src].astype(jnp.float32)
                when(ok, add)
            if slot == OWN:
                rows_at = pl.multiple_of((c % per_head) * chunk, chunk)
                out_q[c // per_head, pl.ds(rows_at, chunk), :] = (part[c % 4, slot] * scale).T.astype(jnp.bfloat16)

                @pl.when(c % per_head == per_head - 1)
                def _():
                    store(c // per_head, 0).start()
            else:
                ret_out[c, slot] = part[c % 4, slot].astype(jnp.bfloat16)
                ret_copy(c, slot, ret_device[slot]).start()
        when(exists(slot), go)

    def exists_dyn(slot):
        a = slot % 3
        ok = jnp.logical_or(a != 0, has_m)
        ok = both(ok, jnp.logical_or(a != 2, has_p))
        return both(ok, jnp.logical_or(slot // 3 != 2, has_xi))

    def relay_1(c):
        relay(c, OTHER_0)
        relay(c, OTHER_M)

    events = (
        (RET_OTHER_P, lambda c: hand_back(c, OTHER_P)), (RET_OTHER_M, lambda c: hand_back(c, OTHER_M)),
        (SEND_OWN, send_own), (RELAY_1, relay_1), (RELAY_2, lambda c: relay(c, SAME_M)),
        (RELAY_3, lambda c: relay(c, OTHER_P)), (MERGE, merge),
        (RET_SAME_M, lambda c: hand_back(c, SAME_M)), (RET_OTHER_0, lambda c: hand_back(c, OTHER_0)),
        (RET_OWN, lambda c: hand_back(c, OWN)), (STORE_KV, store_kv), (DRAIN, drain),
    )

    def place(it, b, offset):
        late = b < offset % SLOTS
        c = it - offset // SLOTS - late.astype(jnp.int32)
        index = b - offset % SLOTS + jnp.where(late, SLOTS, 0)
        return c, index, both(c >= 0, c < chunks)

    for slot in range(SLOTS):
        if slot != OWN:
            when(exists(slot), lambda slot=slot: mark_copy(slot).start())

    def step(it, b):
        for k in range(SLOTS):
            here = [(offset // SLOTS, fn) for offset, fn in events if offset % SLOTS == k]

            def run(here=here):
                for lag, fn in here:
                    c = it - lag
                    pl.when(both(c >= 0, c < chunks))(lambda fn=fn, c=c: fn(c))

            if here:
                pl.when(b == k)(run)

        @pl.when(both(it == SET_UP // SLOTS, b == SET_UP % SLOTS))
        def _():
            for copy in loads[2 * chunks:]:
                copy.wait()
            for h in range(heads):
                keys_t[h] = keys[h].T
            acc_k[...] = jnp.zeros_like(acc_k)
            acc_v[...] = jnp.zeros_like(acc_v)
            take_marks()

        c1, i1, ok1 = place(it, b, FIRST)
        b1 = pick(FIRST_ORDER, i1)

        @pl.when(both(ok1, exists_dyn(b1)))
        def _():
            @pl.when(jnp.logical_or(b1 == SAME_P, b1 >= CROSS_M))
            def _():
                local_wait(fwd, fwd_r, c1, b1)

            first_pass(c1, b1)

            @pl.when(b1 != OWN)
            def _():
                st_copy(c1, b1).start()

        c2, i2, ok2 = place(it, b, SECOND)
        b2 = pick(SECOND_ORDER, i2)

        @pl.when(both(ok2, exists_dyn(b2)))
        def _():
            @pl.when(b2 != OWN)
            def _():
                local_wait(bc_in, bc_r, c2, b2)

            second_pass(c2, b2)

            @pl.when(jnp.logical_or(b2 == SAME_P, b2 >= CROSS_M))
            def _():
                ret_copy(c2, b2, {"tm": jnp.where(b2 == SAME_P, t + s, t - 2 * s), "row": r}).start()

    def chunk_steps(it, carry):
        def one(b, carry):
            step(it, b)
            return carry
        return lax.fori_loop(0, SLOTS, one, carry)

    lax.fori_loop(0, chunks + DRAIN // SLOTS, chunk_steps, 0)

    for slot in range(SLOTS):
        if slot != OWN:
            when(exists(slot), lambda slot=slot: mark_copy(slot).wait_send())
    for h in range(heads):
        for n in range(3):
            store(h, n).wait()


def per_device(times, rows, query, key_tiles, value_tiles, grad_out, neighbours):
    _, _, count, tile, channels = query.shape
    heads = channels // HD
    tokens = count * tile
    per_head = 3
    chunk = tokens // per_head
    chunks = heads * per_head
    entries = neighbours[0, 0]
    slots = jnp.arange(SLOTS, dtype=jnp.int32)
    place = 3 * ((slots // 3 + 1) % 3 - 1) + slots % 3 - 1
    code = 4 + place * (1 - 2 * (lax.axis_index("tm") % 2))
    names = code[:, None] * count + jnp.arange(count * count, dtype=jnp.int32) % count
    listed = jnp.any(names[:, :, None] == jnp.repeat(entries, count, axis=0)[None], axis=2)
    marks = jnp.broadcast_to(listed.astype(jnp.float32)[:, :, None], (SLOTS, count * count, chunk // 2))

    flat = [value.reshape(tokens, channels) for value in (query, key_tiles, value_tiles, grad_out)]
    out = jax.ShapeDtypeStruct((tokens, channels), jnp.bfloat16)
    dma = pltpu.SemaphoreType.DMA
    vmem = pltpu.VMEM
    small = (chunks, SLOTS, 2, chunk)
    grads = pl.pallas_call(
        functools.partial(kernel, times, rows, heads, tile),
        out_shape=(out, out, out),
        in_specs=[pl.BlockSpec(memory_space=pl.ANY)] * 4 + [pl.BlockSpec(memory_space=pltpu.VMEM)],
        out_specs=[pl.BlockSpec(memory_space=pl.ANY)] * 3,
        scratch_shapes=[
            vmem((chunks, SLOTS, 2, chunk, HD), jnp.bfloat16),
            vmem((heads, tokens, HD), jnp.bfloat16),
            vmem((heads, tokens, HD), jnp.bfloat16),
            vmem((heads, HD, tokens), jnp.bfloat16),
            vmem((heads, tokens, HD), jnp.float32),
            vmem((heads, tokens, HD), jnp.float32),
            vmem((4, SLOTS, HD, chunk), jnp.float32),
            vmem((chunks, SLOTS, HD, chunk), jnp.bfloat16),
            vmem((chunks, SLOTS, HD, chunk), jnp.bfloat16),
            vmem(small, jnp.float32),
            vmem(small, jnp.float32),
            vmem((chunks, 1, 2, chunk), jnp.float32),
            vmem(small, jnp.float32),
            vmem((heads, tokens, HD), jnp.bfloat16),
            vmem((heads, tokens, HD), jnp.bfloat16),
            vmem((heads, tokens, HD), jnp.bfloat16),
            dma((2 * chunks + 2 * heads,)),
        ] + [dma((chunks, SLOTS))] * 8 + [vmem((tokens, chunk), jnp.bfloat16)] * 2 + [
            vmem((SLOTS, count * count, chunk // 2), jnp.float32),
            vmem((per_head, SLOTS, 2, chunk), jnp.float32),
            dma((SLOTS,)),
            dma((SLOTS,)),
            dma((heads, 3)),
        ],
        compiler_params=pltpu.CompilerParams(
            collective_id=0, has_side_effects=True, vmem_limit_bytes=56 * 1024 * 1024
        ),
    )(flat[0], flat[1], flat[2], flat[3], marks)
    return tuple(grad.reshape(query.shape) for grad in grads)


def solution(mesh):
    spec = P("tm", "row", None, None, "head")
    return jax.shard_map(
        functools.partial(per_device, mesh.shape["tm"], mesh.shape["row"]),
        mesh=mesh,
        in_specs=(spec, spec, spec, spec, P("tm", "row", None, None)),
        out_specs=(spec, spec, spec),
        check_vma=False,
    )
```
